32 devices in a mesh: parts: 2 (over x), scan: 16 (over z, y, core).
Axes of the slice: x: 2, y: 2, z: 4, core: 2. Of those that a mesh axis runs over, the one named last changes fastest.
Arguments:
- object_slices: float32 [4, 2, 4096, 256], P('parts', None, 'scan'), parts along dimension 0, may hold values from -4 to 4
- probe_modes: float32 [8, 2, 128, 128], P('parts'), parts along dimension 0, may hold values from -4 to 4
- propagator_phase: float32 [128, 128], replicated, may hold values from -3.140625 to 3.140625
- measured: float32 [256, 128, 128], P(('parts', 'scan')), parts along dimension 0, may hold values from 0.5 to 3
- positions: int32 [256, 2], P(('parts', 'scan')), parts along dimension 0, may hold values from 0 to 3839, as said below
- live_count: int32 [32], P(('parts', 'scan')), parts along dimension 0, may hold values from 1 to 8, as said below
Outputs:
- object_gradient: float32 [4, 2, 4096, 256], P('parts', None, 'scan'), parts along dimension 0
- probe_gradient: float32 [8, 2, 128, 128], P('parts'), parts along dimension 0
- position_loss: float32 [256], P(('parts', 'scan')), parts along dimension 0
The draws below stay inside these ranges and needn't reach their ends.
There are 2 independent parts, one for each index of `parts`. The reference program is written for one: setup_inputs(seed, part) draws one part's arguments, and reference() takes and returns one part's arrays. A program takes and returns all parts, laid end to end along the dimension named above; an argument that names none is the same for every part. Nothing has to cross between parts.
Inputs may be any that keep to these rules, and one draw needn't show every extreme that they name: `positions`: object tile k is rows k * 256 to (k + 1) * 256 - 1. Slots s * 8 to (s + 1) * 8 - 1 belong to scan owner s; each of their windows lies within tiles s - 2 to s + 2 and never in the last tile alone; columns start at 0 to 128. Every owner has a slot in tile max(s - 2, 0) and a slot whose window reaches tile min(s + 2, 16 - 1). `live_count`: live slots of an owner come first; some owner is full in every draw.
All inputs are finite; a program needn't handle non-finite values.
Results may differ from the reference program's by a relative error of at most 0.0003.
Values sent between devices are 32-bit elements; how exact they have to be, the bound alone decides.
No kernel may reach another device: no remote copies, remote signals or barrier semaphores. Data moves between devices by JAX's collectives and lax.ppermute only.
A program may use at most 128 MiB of HBM per device.

```python
import jax
import jax.numpy as jnp
from jax import lax

PATCH = 128
MODES = 4
SLICES = 2
REACH = 2
TILE_ROWS = 256
COLS = 256
POS_DEV = 8
NROWS = 4096
POSITIONS = 128
N_SCAN = 16


def draw_live_count(key, part):
    key = jax.random.fold_in(key, 11)
    key_counts, key_busy = jax.random.split(key)
    counts = jax.random.randint(key_counts, (N_SCAN,), 1, POS_DEV + 1)
    busiest = jax.random.randint(key_busy, (), 0, N_SCAN)
    filled = jnp.where(jnp.arange(N_SCAN) == busiest, POS_DEV, counts)
    return filled.astype(jnp.int32)


def draw_positions(key, part):
    key = jax.random.fold_in(key, 23)
    key_list = jax.random.split(key, 5)
    owner_ids = jnp.repeat(jnp.arange(N_SCAN), POS_DEV)
    slot_ids = jnp.tile(jnp.arange(POS_DEV), N_SCAN)
    lowest = jnp.maximum(owner_ids - REACH, 0)
    highest = jnp.minimum(owner_ids + REACH - 1, N_SCAN - 2)
    spread = highest - lowest + 1
    tile_pick = lowest + jax.random.randint(key_list[0], (POSITIONS,), 0, 1 << 20) % spread
    row_offset = jax.random.randint(key_list[1], (POSITIONS,), 0, TILE_ROWS)
    col_start = jax.random.randint(key_list[2], (POSITIONS,), 0, COLS - PATCH + 1)
    low_slot = jax.random.randint(key_list[3], (N_SCAN,), 0, POS_DEV)
    high_slot = (low_slot + 1 + jax.random.randint(key_list[4], (N_SCAN,), 0, POS_DEV - 1)) % POS_DEV
    is_low = slot_ids == low_slot[owner_ids]
    is_high = slot_ids == high_slot[owner_ids]
    tile_pick = jnp.where(is_low, lowest, jnp.where(is_high, highest, tile_pick))
    first_corner = is_low & (owner_ids == 0)
    row_offset = jnp.where(is_high, TILE_ROWS - 1, jnp.where(first_corner, 0, row_offset))
    col_start = jnp.where(first_corner, 0, col_start)
    row_start = tile_pick * TILE_ROWS + row_offset
    return jnp.stack([row_start, col_start], axis=1).astype(jnp.int32)


def level_of(key, dims, shards, least, top_value):
    def one(position, blocks):
        draws = jax.random.uniform(jax.random.fold_in(jax.random.fold_in(key, 6), position), (blocks,), jnp.float32, least / len(shards), top_value / len(shards))
        return jnp.repeat(jnp.exp(draws), dims[position] // blocks).reshape((-1,) + (1,) * (len(dims) - position - 1))

    level = one(*shards[0])
    for cut in shards[1:]:
        level = level * one(*cut)
    return level


def normal_values(own_key, extent, scale, most, shards=(), held_as=jnp.bfloat16):
    entries = scale * jax.random.normal(own_key, extent, jnp.float32)
    if shards:
        entries = entries * level_of(own_key, extent, shards, -0.22, 0.18)
    return jnp.clip(entries, -most, most).astype(held_as)


def setup_inputs(seed: int = 0, part: int = 0) -> dict:
    seeds = jax.random.split(jax.random.key(seed), 7)
    part_keys = jax.random.split(jax.random.fold_in(seeds[6], part), 7)
    object_slices = normal_values(part_keys[0], (SLICES, 2, NROWS, COLS), 0.7, 4.0, ((2, 16),), jnp.float32)
    probe_modes = normal_values(part_keys[1], (MODES, 2, PATCH, PATCH), 0.5, 4.0, (), jnp.float32)
    propagator_phase = jnp.clip(jax.random.uniform(seeds[2], (PATCH, PATCH), jnp.float32, -3.140625, 3.140625), -3.140625, 3.140625)
    measured = jnp.clip(0.5 + 2.5 * jax.random.uniform(part_keys[3], (POSITIONS, PATCH, PATCH), jnp.float32) ** level_of(part_keys[3], (POSITIONS, PATCH, PATCH), ((0, 16),), -0.2, 0.2), 0.5, 3.0)
    positions = draw_positions(jax.random.fold_in(jax.random.fold_in(seeds[6], part), 71), part)
    live_count = draw_live_count(jax.random.fold_in(jax.random.fold_in(seeds[6], part), 71), part)
    return dict(object_slices=object_slices, probe_modes=probe_modes, propagator_phase=propagator_phase, measured=measured, positions=positions, live_count=live_count)


def slot_loss(cell_values, mode_values, propagator_phase, target):
    propagator = lax.complex(jnp.cos(propagator_phase), jnp.sin(propagator_phase))
    wave = lax.complex(mode_values[:, 0], mode_values[:, 1])
    for depth in range(SLICES):
        transmission = lax.complex(cell_values[depth, 0], cell_values[depth, 1])
        if depth > 0:
            spectrum = jnp.fft.fft2(wave, norm='ortho') * propagator
            wave = jnp.fft.ifft2(spectrum, norm='ortho')
        wave = wave * transmission
    far_field = jnp.fft.fft2(wave, norm='ortho')
    intensity = lax.optimization_barrier(jnp.sum(jnp.real(far_field) ** 2 + jnp.imag(far_field) ** 2, axis=0))
    amplitude = jnp.sqrt(intensity + 0.5)
    residual_cells = amplitude - target
    return 0.5 * jnp.sum(residual_cells * residual_cells)

def reference(object_slices, probe_modes, propagator_phase, measured, positions, live_count):
    anchor = jnp.zeros((), jnp.int32)

    def visit(carry, position_id):
        grad_total, mode_total = carry
        row_start = positions[position_id, 0]
        col_start = positions[position_id, 1]
        live_slots = live_count[position_id // POS_DEV]
        weight = jnp.where(position_id % POS_DEV < live_slots, 1.0, 0.0).astype(object_slices.dtype)
        corner = (anchor, anchor, row_start, col_start)
        cells = lax.dynamic_slice(object_slices, corner, (SLICES, 2, PATCH, PATCH))
        target = measured[position_id]

        def local_loss(cell_values, mode_values):
            return slot_loss(cell_values, mode_values, propagator_phase, target)
        loss_value, pullback = jax.vjp(local_loss, cells, probe_modes)
        cell_grad, mode_grad = pullback(jnp.ones_like(loss_value))
        block = lax.dynamic_slice(grad_total, corner, (SLICES, 2, PATCH, PATCH))
        grad_total = lax.dynamic_update_slice(grad_total, block + weight * cell_grad, corner)
        scaled_loss = weight * loss_value * (2.0 / (PATCH * PATCH))
        return ((grad_total, mode_total + weight * mode_grad), scaled_loss)
    start_state = (jnp.zeros_like(object_slices), jnp.zeros_like(probe_modes))
    (grad_total, mode_total), position_loss = lax.scan(visit, start_state, jnp.arange(POSITIONS, dtype=jnp.int32))
    return (grad_total, mode_total, position_loss)
```

```python
import functools
import math

import jax
import jax.numpy as jnp
import numpy as np
from jax import lax
from jax.experimental import pallas as pl
from jax.experimental.pallas import tpu as pltpu
from jax.sharding import PartitionSpec as P

F32 = jnp.float32
BF16 = jnp.bfloat16
LOSS_PAD = 32


def shifted(value, axis, steps):
    count = lax.axis_size(axis)
    first, last = (max(0, -steps), min(count, count - steps))
    return lax.ppermute(value, axis, [(source, source + steps) for source in range(first, last)])


def swapped(value, axis, bit):
    count = lax.axis_size(axis)
    return lax.ppermute(value, axis, [(source, source ^ bit) for source in range(count)])


def tables(size):
    counter = np.arange(size)
    angles = (counter[:, None] * counter[None, :] % size) * (2.0 * math.pi / size)
    cosine = np.cos(angles) / math.sqrt(size)
    sine = np.sin(angles) / math.sqrt(size)
    forward = np.block([[cosine, -sine], [sine, cosine]]).astype(np.float32)
    high = forward.astype(jnp.bfloat16)
    low = (forward - high.astype(np.float32)).astype(jnp.bfloat16)
    right_f = np.concatenate([high, high, low], 0)
    right_g = np.concatenate([high.T, high.T, low.T], 0)
    left_f = np.concatenate([high.T, high.T, low.T], 1)
    left_g = np.concatenate([high, high, low], 1)
    return right_f, right_g, left_f, left_g


def kernel(
    size, modes, slots, tile, place_ref, slot_ref, own_ref, pair_ref, pats, wave_ref, prop_ref,
    rf_ref, rg_ref, lf_ref, lg_ref, mine_ref, theirs_ref, modegrad_ref,
    obj, acc, pat, cells, cgrad, wave1, far, ops, sem,
):
    core = place_ref[0]
    chip_top = place_ref[1]
    first_id = place_ref[2]
    half = size // 2
    top = lax.mul(core, tile)
    other = tile - top
    top = pl.multiple_of(top, tile)
    other = pl.multiple_of(other, tile)

    copies = []

    def move(source, target):
        copy = pltpu.make_async_copy(source, target, sem.at[len(copies)])
        copy.start()
        copies.append(copy)

    rows = slots * size
    (own_pat, pair_pat, up_own, up_pair, down_own, down_pair) = pats
    move(own_ref, obj.at[:, :, pl.ds(top, tile)])
    move(pair_ref, obj.at[:, :, pl.ds(other, tile)])
    for group, (a, b) in enumerate(((up_own, up_pair), (own_pat, pair_pat), (down_own, down_pair))):
        move(a.at[pl.ds(0, rows)], pat.at[2 * group + core])
        move(b.at[pl.ds(0, rows)], pat.at[2 * group + 1 - core])
    halo_row = rows + 8
    for k in range(2):
        for ri in range(2):
            for side in range(2):
                block = pl.ds(halo_row + ((k * 2 + ri) * 2 + side) * half, half)
                lanes = pl.ds(side * size, size)
                move(
                    down_own.at[block],
                    obj.at[k, ri, pl.ds(pl.multiple_of(2 * tile + core * half, half), half), lanes],
                )
                move(
                    down_pair.at[block],
                    obj.at[k, ri, pl.ds(pl.multiple_of(2 * tile + half - core * half, half), half), lanes],
                )
    acc[...] = jnp.zeros_like(acc)
    modegrad_ref[...] = jnp.zeros_like(modegrad_ref)
    for copy in copies:
        copy.wait()

    mat = functools.partial(jnp.dot, preferred_element_type=F32)
    (r1, l1, l2, r2, r3, l3, l4, r4, r5, l5, l6, r6) = range(12)

    def put_right(stage, m, real, imag):
        hi, lo = ops.at[stage, 0], ops.at[stage, 1]
        for part, value in enumerate((real, imag)):
            high = value.astype(BF16)
            at = (pl.ds(m * size, size), pl.ds(part * size, size))
            hi[at] = high
            lo[at] = (value - high.astype(F32)).astype(BF16)

    def right(stage, m, table):
        at = (pl.ds(m * size, size), pl.ds(0, 2 * size))
        high, low = ops.at[stage, 0][at], ops.at[stage, 1][at]
        out = mat(jnp.concatenate([high, low, high], 1), table[...])
        return out[:, :size], out[:, size:]

    def put_left(stage, m, real, imag):
        hi, lo = ops.at[stage, 0], ops.at[stage, 1]
        base = (m // 2) * 2 * size
        for part, value in enumerate((real, imag)):
            high = value.astype(BF16)
            at = (pl.ds(base + part * size, size), pl.ds((m % 2) * size, size))
            hi[at] = high
            lo[at] = (value - high.astype(F32)).astype(BF16)

    def left(stage, p, table):
        at = (pl.ds(p * 2 * size, 2 * size), pl.ds(0, 2 * size))
        high, low = ops.at[stage, 0][at], ops.at[stage, 1][at]
        out = mat(table[...], jnp.concatenate([high, low, high], 0))
        return [(out[:size, j * size:(j + 1) * size], out[size:, j * size:(j + 1) * size]) for j in range(2)]

    def wave_at(m):
        return (wave_ref[m, 0], wave_ref[m, 1])

    def window(slot, row, column):
        base = pl.multiple_of(lax.div(row, 8) * 8, 8)
        ahead = row - base
        tall = size + 8
        for k in range(2):
            for ri in range(2):
                value = obj[k, ri, pl.ds(base, tall), :]
                value = pltpu.roll(value, 2 * size - column, 1)[:, :size]
                cells[k, ri] = pltpu.roll(value, tall - ahead, 0)[:size]
        for m in range(modes):
            pr, pi = wave_at(m)
            o_r, o_i = cells[0, 0], cells[0, 1]
            put_right(r1, m, pr * o_r - pi * o_i, pr * o_i + pi * o_r)
            put_left(l1, m, *right(r1, m, rf_ref))
        for p in range(modes // 2):
            for j, (re, im) in enumerate(left(l1, p, lf_ref)):
                h_r, h_i = prop_ref[0], prop_ref[1]
                put_left(l2, 2 * p + j, re * h_r - im * h_i, re * h_i + im * h_r)
            for j, (re, im) in enumerate(left(l2, p, lg_ref)):
                put_right(r2, 2 * p + j, re, im)
        for m in range(modes):
            re, im = right(r2, m, rg_ref)
            wave1[m, 0] = re
            wave1[m, 1] = im
            o_r, o_i = cells[1, 0], cells[1, 1]
            put_right(r3, m, re * o_r - im * o_i, re * o_i + im * o_r)
            put_left(l3, m, *right(r3, m, rf_ref))
        total = jnp.zeros((size, size), F32)
        for p in range(modes // 2):
            for j, (re, im) in enumerate(left(l3, p, lf_ref)):
                far[2 * p + j, 0] = re
                far[2 * p + j, 1] = im
                total = total + (re * re + im * im)
        target = pat[slot // slots, pl.ds(pl.multiple_of((slot % slots) * size, size), size), :]
        amplitude = jnp.sqrt(total + 0.5)
        residual = amplitude - target
        loss = 0.5 * jnp.sum(residual * residual) * (2.0 / (size * size))
        ratio = residual / amplitude
        at = (pl.ds(2 * modes * size, 8), pl.ds(0, size))
        place = lax.broadcasted_iota(jnp.int32, (8, size), 0) * size + lax.broadcasted_iota(jnp.int32, (8, size), 1)
        modegrad_ref[at] = jnp.where(place == first_id + slot, loss, modegrad_ref[at])
        for p in range(modes // 2):
            for m in (2 * p, 2 * p + 1):
                put_left(l4, m, far[m, 0] * ratio, far[m, 1] * ratio)
            for j, (re, im) in enumerate(left(l4, p, lg_ref)):
                put_right(r4, 2 * p + j, re, im)
        for m in range(modes):
            re, im = right(r4, m, rg_ref)
            w_r, w_i = wave1[m, 0], wave1[m, 1]
            add_r, add_i = re * w_r + im * w_i, im * w_r - re * w_i
            if m == 0:
                cgrad[1, 0] = add_r
                cgrad[1, 1] = add_i
            else:
                cgrad[1, 0] += add_r
                cgrad[1, 1] += add_i
            o_r, o_i = cells[1, 0], cells[1, 1]
            put_right(r5, m, re * o_r + im * o_i, im * o_r - re * o_i)
            put_left(l5, m, *right(r5, m, rf_ref))
        for p in range(modes // 2):
            for j, (re, im) in enumerate(left(l5, p, lf_ref)):
                h_r, h_i = prop_ref[0], prop_ref[1]
                put_left(l6, 2 * p + j, re * h_r + im * h_i, im * h_r - re * h_i)
            for j, (re, im) in enumerate(left(l6, p, lg_ref)):
                put_right(r6, 2 * p + j, re, im)
        for m in range(modes):
            re, im = right(r6, m, rg_ref)
            o_r, o_i = cells[0, 0], cells[0, 1]
            modegrad_ref[pl.ds(2 * m * size, size), :] += re * o_r + im * o_i
            modegrad_ref[pl.ds((2 * m + 1) * size, size), :] += im * o_r - re * o_i
            pr, pi = wave_at(m)
            add_r, add_i = re * pr + im * pi, im * pr - re * pi
            if m == 0:
                cgrad[0, 0] = add_r
                cgrad[0, 1] = add_i
            else:
                cgrad[0, 0] += add_r
                cgrad[0, 1] += add_i
        for k in range(2):
            for ri in range(2):
                value = jnp.concatenate([cgrad[k, ri], jnp.zeros((8, size), F32)], 0)
                value = pltpu.roll(value, ahead, 0)
                value = jnp.concatenate([value, jnp.zeros_like(value)], 1)
                acc[k, ri, pl.ds(base, tall), :] += pltpu.roll(value, column, 1)

    def visit(slot, count):
        row = slot_ref[slot, 0] - chip_top
        here = jnp.logical_and(slot_ref[slot, 2] > 0, jnp.logical_and(row >= 0, row < 2 * tile))

        @pl.when(jnp.logical_and(here, lax.rem(count, 2) == core))
        def _():
            window(slot, row, slot_ref[slot, 1])

        return count + here.astype(jnp.int32)

    lax.fori_loop(0, 6 * slots, visit, jnp.int32(0))

    copies.clear()
    move(acc.at[:, :, pl.ds(top, tile)], mine_ref)
    move(acc.at[:, :, pl.ds(other, tile)], theirs_ref.at[:, :, pl.ds(0, tile)])
    move(acc.at[:, :, pl.ds(2 * tile, size)], theirs_ref.at[:, :, pl.ds(tile, size)])
    for copy in copies:
        copy.wait()


def flat_kernel(size, modes, slots, tile, *refs):
    place_ref, slot_ref, own_ref, pair_ref = refs[:4]
    kernel(size, modes, slots, tile, place_ref, slot_ref, own_ref, pair_ref, refs[4:10], *refs[10:])


def all_windows(place, slot_list, own, pair, pats, waves, prop, slots):
    modes, _, size, _ = waves.shape
    tile = own.shape[2]
    columns = own.shape[3]
    rf, rg, lf, lg = (jnp.asarray(t) for t in tables(size))
    total_rows = 2 * modes * size + LOSS_PAD
    hbm = pl.BlockSpec(memory_space=pl.ANY)
    vmem = pl.BlockSpec(memory_space=pltpu.VMEM)
    smem = pl.BlockSpec(memory_space=pltpu.SMEM)
    return pl.pallas_call(
        functools.partial(flat_kernel, size, modes, slots, tile),
        out_shape=(
            jax.ShapeDtypeStruct((2, 2, tile, columns), F32),
            jax.ShapeDtypeStruct((2, 2, tile + size, columns), F32),
            jax.ShapeDtypeStruct((total_rows, size), F32),
        ),
        in_specs=[smem, smem, hbm, hbm] + [hbm] * 6 + [vmem] * 6,
        out_specs=(hbm, hbm, vmem),
        scratch_shapes=[
            pltpu.VMEM((2, 2, 2 * tile + size, columns), F32),
            pltpu.VMEM((2, 2, 2 * tile + size, columns), F32),
            pltpu.VMEM((6, slots * size, size), F32),
            pltpu.VMEM((2, 2, size, size), F32),
            pltpu.VMEM((2, 2, size, size), F32),
            pltpu.VMEM((modes, 2, size, size), F32),
            pltpu.VMEM((modes, 2, size, size), F32),
            pltpu.VMEM((12, 2, modes * size, 2 * size), BF16),
            pltpu.SemaphoreType.DMA((24,)),
        ],
        compiler_params=pltpu.CompilerParams(vmem_limit_bytes=48 * 1024 * 1024),
    )(place, slot_list, own, pair, *pats, waves, prop, rf, rg, lf, lg)


def sum_over(value, axis):
    count = lax.axis_size(axis)
    index = lax.axis_index(axis)
    bits = [1 << i for i in range(count.bit_length() - 1)]
    split, whole = bits[:2], bits[2:]
    for bit in split:
        half = value.shape[0] // 2
        side = (index // bit) % 2
        kept = lax.dynamic_slice_in_dim(value, side * half, half, 0)
        given = lax.dynamic_slice_in_dim(value, (1 - side) * half, half, 0)
        value = kept + swapped(given, axis, bit)
    for bit in whole:
        value = value + swapped(value, axis, bit)
    for bit in split[::-1]:
        side = (index // bit) % 2
        got = swapped(value, axis, bit)
        value = jnp.concatenate([jnp.where(side == 0, value, got), jnp.where(side == 0, got, value)], 0)
    return value


def shards(object_slices, probe_modes, propagator_phase, measured, positions, live_count):
    modes, _, size, _ = probe_modes.shape
    tile = object_slices.shape[2]
    slots = positions.shape[0]
    index = lax.axis_index("scan")
    core = index % 2
    chip = index // 2
    prop = jnp.stack([jnp.cos(propagator_phase), jnp.sin(propagator_phase)])
    live = jnp.arange(slots, dtype=jnp.int32) < live_count[0]
    facts = jnp.concatenate([positions, live.astype(jnp.int32)[:, None]], 1).astype(F32)
    facts = jnp.pad(facts, ((0, 0), (0, size - 3)))
    own_pat = jnp.concatenate([measured.reshape(slots * size, size), facts], 0)
    up_own = shifted(own_pat, "scan", 2)
    pair = swapped(object_slices, "scan", 1)
    half = size // 2
    first = jnp.where(core == 0, object_slices[:, :, :half], pair[:, :, half:size])
    blocks = [first[k, ri, :, s * size:(s + 1) * size] for k in range(2) for ri in range(2) for s in range(2)]
    down_own = shifted(jnp.concatenate([own_pat] + blocks, 0), "scan", -2)
    pair_pat = swapped(own_pat, "scan", 1)
    up_pair = swapped(up_own, "scan", 1)
    down_pair = swapped(down_own, "scan", 1)
    rows = slots * size
    lists = []
    for a, b in ((up_own, up_pair), (own_pat, pair_pat), (down_own, down_pair)):
        a, b = a[rows:rows + slots, :3], b[rows:rows + slots, :3]
        lists += [jnp.where(core == 0, a, b), jnp.where(core == 0, b, a)]
    slot_list = jnp.concatenate(lists, 0).astype(jnp.int32)
    place = jnp.stack([core, chip * 2 * tile, (chip - 1) * 2 * slots]).astype(jnp.int32)
    mine, theirs, sums = all_windows(
        place, slot_list, object_slices, pair,
        (own_pat, pair_pat, up_own, up_pair, down_own, down_pair), probe_modes, prop, slots,
    )
    back = swapped(theirs, "scan", 1)
    halo = theirs[:, :, tile:] + back[:, :, tile:]
    count = lax.axis_size("scan")
    halo = lax.ppermute(halo, "scan", [(s, s + 1) for s in range(1, count - 1, 2)])
    sums = sum_over(sums, "scan")
    grad = mine + back[:, :, :tile] + jnp.pad(halo, ((0, 0), (0, 0), (0, tile - size), (0, 0)))
    mode_rows = 2 * modes * size
    probe_gradient = sums[:mode_rows].reshape(probe_modes.shape)
    losses = sums[mode_rows:mode_rows + 8].reshape(-1)
    position_loss = lax.dynamic_slice_in_dim(losses, index * slots, slots, 0)
    return (grad, probe_gradient, position_loss)


def solution(mesh):
    return jax.shard_map(
        shards,
        mesh=mesh,
        in_specs=(
            P("parts", None, "scan", None),
            P("parts", None, None, None),
            P(),
            P(("parts", "scan"), None, None),
            P(("parts", "scan"), None),
            P(("parts", "scan")),
        ),
        out_specs=(
            P("parts", None, "scan", None),
            P("parts", None, None, None),
            P(("parts", "scan")),
        ),
        check_vma=False,
    )
```

```python
import functools
import math

import jax
import jax.numpy as jnp
import numpy as np
from jax import lax
from jax.experimental import pallas as pl
from jax.experimental.pallas import tpu as pltpu
from jax.sharding import PartitionSpec as P

F32 = jnp.float32
BF16 = jnp.bfloat16
LOSS_PAD = 32
HBM = pl.BlockSpec(memory_space=pl.ANY)
VMEM = pl.BlockSpec(memory_space=pltpu.VMEM)
SMEM = pl.BlockSpec(memory_space=pltpu.SMEM)


def shifted(value, axis, steps):
    count = lax.axis_size(axis)
    first, last = (max(0, -steps), min(count, count - steps))
    return lax.ppermute(value, axis, [(source, source + steps) for source in range(first, last)])


def swapped(value, axis, bit):
    count = lax.axis_size(axis)
    return lax.ppermute(value, axis, [(source, source ^ bit) for source in range(count)])


def fourier_table(size):
    counter = np.arange(size)
    angles = (counter[:, None] * counter[None, :] % size) * (2.0 * math.pi / size)
    return np.stack([np.cos(angles), np.sin(angles)]).astype(np.float32) / np.float32(math.sqrt(size))


class Mover:
    def __init__(self, sem):
        self.sem, self.copies, self.used = sem, [], 0

    def __call__(self, source, target):
        copy = pltpu.make_async_copy(source, target, self.sem.at[self.used])
        copy.start()
        self.copies.append(copy)
        self.used += 1

    def wait(self):
        for copy in self.copies:
            copy.wait()
        self.copies = []


def pack_up_kernel(slots, corners, live, measured, out):
    rows, size = measured.shape
    out[:rows] = measured[...]
    lane = lax.broadcasted_iota(jnp.int32, (8, size), 1)
    line = lax.broadcasted_iota(jnp.int32, (8, size), 0)
    value = jnp.zeros((8, size), jnp.int32)
    for s in range(slots):
        alive = (live[0] > s).astype(jnp.int32)
        fact = jnp.where(lane == 0, corners[0, s], jnp.where(lane == 1, corners[1, s], alive))
        value = jnp.where(jnp.logical_and(line == s, lane < 3), fact, value)
    out[rows:] = value.astype(F32)


def pack_down_kernel(place, up, own, pair, out, sem):
    rows, size = up.shape
    half = size // 2
    core = place[0]
    for source, side in ((own, 0), (pair, 1)):

        @pl.when(core == side)
        def _():
            move = Mover(sem)
            for k in range(2):
                for ri in range(2):
                    for lanes in range(2):
                        block = pl.ds(rows + ((k * 2 + ri) * 2 + lanes) * half, half)
                        move(source.at[k, ri, pl.ds(side * half, half), pl.ds(lanes * size, size)], out.at[block])
            out[:rows] = up[...]
            move.wait()


def pack_up(positions, live, measured):
    slots, _, size = measured.shape
    return pl.pallas_call(
        functools.partial(pack_up_kernel, slots),
        out_shape=jax.ShapeDtypeStruct((slots * size + 8, size), F32),
        in_specs=[SMEM, SMEM, VMEM],
        out_specs=VMEM,
    )(positions.T, live, measured.reshape(slots * size, size))


def pack_down(place, up, own, pair):
    rows, size = up.shape
    return pl.pallas_call(
        pack_down_kernel,
        out_shape=jax.ShapeDtypeStruct((rows + 4 * size, size), F32),
        in_specs=[SMEM, VMEM, HBM, HBM],
        out_specs=VMEM,
        scratch_shapes=[pltpu.SemaphoreType.DMA((8,))],
    )(place, up, own, pair)


def kernel(
    size, modes, slots, tile, final, place, own, pair, pats, before, wave_ref, prop_ref, table_ref, outs, sums_ref,
    obj, acc, pat, facts, todo, tables, cells, cgrad, wave1, far, ops, sem,
):
    core = place[0]
    chip_top = place[1]
    first_id = place[2]
    half = size // 2
    rows = slots * size
    top = pl.multiple_of(core * tile, tile)
    other = pl.multiple_of(tile - core * tile, tile)
    limit = 2 * tile - size
    first_group = 0 if final else 1

    move = Mover(sem)
    for i, source in enumerate(pats):
        move(source.at[pl.ds(rows, 8)], facts.at[i])
    facts_in = move.copies
    move.copies = []
    move(own, obj.at[:, :, pl.ds(top, tile)])
    move(pair, obj.at[:, :, pl.ds(other, tile)])
    for i, source in enumerate(pats):
        move(source.at[pl.ds(0, rows)], pat.at[i])
    if final:
        for k in range(2):
            for ri in range(2):
                for side in range(2):
                    block = pl.ds(rows + 8 + ((k * 2 + ri) * 2 + side) * half, half)
                    lanes = pl.ds(side * size, size)
                    near = pl.multiple_of(2 * tile + core * half, half)
                    far_off = pl.multiple_of(2 * tile + half - core * half, half)
                    move(pats[4].at[block], obj.at[k, ri, pl.ds(near, half), lanes])
                    move(pats[5].at[block], obj.at[k, ri, pl.ds(far_off, half), lanes])
        old_grad, old_sums = before
        move(old_grad, acc.at[:, :, pl.ds(0, 2 * tile)])
        move(old_sums, sums_ref)
        acc[:, :, 2 * tile:] = jnp.zeros((2, 2, size, acc.shape[3]), F32)
    else:
        acc[...] = jnp.zeros_like(acc)
        sums_ref[...] = jnp.zeros_like(sums_ref)

    right_f, right_g, left_f, left_g = (tables.at[i] for i in range(4))
    cosine, sine = table_ref[0], table_ref[1]
    for index, part in enumerate(("high", "high", "low")):
        def cut(value):
            high = value.astype(BF16)
            return high if part == "high" else (value - high.astype(F32)).astype(BF16)
        c, s, n = cut(cosine), cut(sine), cut(-sine)
        base = index * 2 * size
        one, two = pl.ds(0, size), pl.ds(size, size)
        for kind, (a, b, d, e) in ((0, (c, n, s, c)), (1, (c, s, n, c))):
            tables[kind, pl.ds(base, size), one] = a
            tables[kind, pl.ds(base, size), two] = b
            tables[kind, pl.ds(base + size, size), one] = d
            tables[kind, pl.ds(base + size, size), two] = e

    def square(kind, part):
        return tables[kind, pl.ds(part * 2 * size, 2 * size), :]

    mat = functools.partial(jnp.dot, preferred_element_type=F32)
    (r1, l1, l2, r2, r3, l3, l4, r4, r5, l5, l6, r6) = range(12)
    pairs = range(modes // 2)

    def split(b, stage, at, value):
        high = value.astype(BF16)
        ops.at[b, stage, 0][at] = high
        ops.at[b, stage, 1][at] = (value - high.astype(F32)).astype(BF16)

    def put_right(b, stage, m, real, imag):
        split(b, stage, (pl.ds(m * size, size), pl.ds(0, size)), real)
        split(b, stage, (pl.ds(m * size, size), pl.ds(size, size)), imag)

    def right(b, stage, m, kind):
        at = (pl.ds(m * size, size), pl.ds(0, 2 * size))
        high, low = ops.at[b, stage, 0][at], ops.at[b, stage, 1][at]
        out = mat(jnp.concatenate([high, low, high], 1), tables[kind])
        return out[:, :size], out[:, size:]

    def put_left(b, stage, m, real, imag):
        base = (m // 2) * 2 * size
        lanes = pl.ds((m % 2) * size, size)
        split(b, stage, (pl.ds(base, size), lanes), real)
        split(b, stage, (pl.ds(base + size, size), lanes), imag)

    def left(b, stage, p, kind):
        at = (pl.ds(p * 2 * size, 2 * size), pl.ds(0, 2 * size))
        high, low = ops.at[b, stage, 0][at], ops.at[b, stage, 1][at]
        wide = jnp.concatenate([square(1 - kind, 0), square(1 - kind, 0), square(1 - kind, 2)], 1)
        out = mat(wide, jnp.concatenate([high, low, high], 0))
        return [(out[:size, j * size:(j + 1) * size], out[size:, j * size:(j + 1) * size]) for j in range(2)]

    def where_of(slot):
        group, owner, place_in = slot // (2 * slots), (slot // slots) % 2, slot % slots
        return 2 * (group - first_group) + (owner + core - 2 * owner * core), place_in

    def fact(slot, which):
        buffer, line = where_of(slot)
        return facts[buffer, line, which].astype(jnp.int32)

    def window(b, slot):
        row = fact(slot, 0) - chip_top
        column = fact(slot, 1)
        base = pl.multiple_of(lax.div(row, 8) * 8, 8)
        ahead = row - base
        tall = size + 8
        for k in range(2):
            for ri in range(2):
                value = obj[k, ri, pl.ds(base, tall), :]
                value = pltpu.roll(value, 2 * size - column, 1)[:, :size]
                cells[b, k, ri] = pltpu.roll(value, tall - ahead, 0)[:size]
        yield
        for m in range(modes):
            pr, pi = wave_ref[m, 0], wave_ref[m, 1]
            o_r, o_i = cells[b, 0, 0], cells[b, 0, 1]
            put_right(b, r1, m, pr * o_r - pi * o_i, pr * o_i + pi * o_r)
        yield
        for m in range(modes):
            put_left(b, l1, m, *right(b, r1, m, 0))
        yield
        for p in pairs:
            for j, (re, im) in enumerate(left(b, l1, p, 0)):
                h_r, h_i = prop_ref[0], prop_ref[1]
                put_left(b, l2, 2 * p + j, re * h_r - im * h_i, re * h_i + im * h_r)
        yield
        for p in pairs:
            for j, (re, im) in enumerate(left(b, l2, p, 1)):
                put_right(b, r2, 2 * p + j, re, im)
        yield
        for m in range(modes):
            re, im = right(b, r2, m, 1)
            wave1[b, m, 0] = re
            wave1[b, m, 1] = im
            o_r, o_i = cells[b, 1, 0], cells[b, 1, 1]
            put_right(b, r3, m, re * o_r - im * o_i, re * o_i + im * o_r)
        yield
        for m in range(modes):
            put_left(b, l3, m, *right(b, r3, m, 0))
        yield
        total = jnp.zeros((size, size), F32)
        for p in pairs:
            for j, (re, im) in enumerate(left(b, l3, p, 0)):
                far[b, 2 * p + j, 0] = re
                far[b, 2 * p + j, 1] = im
                total = total + (re * re + im * im)
        yield
        buffer, line = where_of(slot)
        target = pat[buffer, pl.ds(pl.multiple_of(line * size, size), size), :]
        amplitude = jnp.sqrt(total + 0.5)
        residual = amplitude - target
        loss = 0.5 * jnp.sum(residual * residual) * (2.0 / (size * size))
        ratio = residual / amplitude
        at = (pl.ds(2 * modes * size, 8), pl.ds(0, size))
        spot = lax.broadcasted_iota(jnp.int32, (8, size), 0) * size + lax.broadcasted_iota(jnp.int32, (8, size), 1)
        sums_ref[at] = jnp.where(spot == first_id + slot, loss, sums_ref[at])
        for m in range(modes):
            put_left(b, l4, m, far[b, m, 0] * ratio, far[b, m, 1] * ratio)
        yield
        for p in pairs:
            for j, (re, im) in enumerate(left(b, l4, p, 1)):
                put_right(b, r4, 2 * p + j, re, im)
        yield
        for m in range(modes):
            re, im = right(b, r4, m, 1)
            w_r, w_i = wave1[b, m, 0], wave1[b, m, 1]
            add_r, add_i = re * w_r + im * w_i, im * w_r - re * w_i
            if m == 0:
                cgrad[b, 1, 0] = add_r
                cgrad[b, 1, 1] = add_i
            else:
                cgrad[b, 1, 0] += add_r
                cgrad[b, 1, 1] += add_i
            o_r, o_i = cells[b, 1, 0], cells[b, 1, 1]
            put_right(b, r5, m, re * o_r + im * o_i, im * o_r - re * o_i)
        yield
        for m in range(modes):
            put_left(b, l5, m, *right(b, r5, m, 0))
        yield
        for p in pairs:
            for j, (re, im) in enumerate(left(b, l5, p, 0)):
                h_r, h_i = prop_ref[0], prop_ref[1]
                put_left(b, l6, 2 * p + j, re * h_r + im * h_i, im * h_r - re * h_i)
        yield
        for p in pairs:
            for j, (re, im) in enumerate(left(b, l6, p, 1)):
                put_right(b, r6, 2 * p + j, re, im)
        yield
        for m in range(modes):
            re, im = right(b, r6, m, 1)
            o_r, o_i = cells[b, 0, 0], cells[b, 0, 1]
            sums_ref[pl.ds(2 * m * size, size), :] += re * o_r + im * o_i
            sums_ref[pl.ds((2 * m + 1) * size, size), :] += im * o_r - re * o_i
            pr, pi = wave_ref[m, 0], wave_ref[m, 1]
            add_r, add_i = re * pr + im * pi, im * pr - re * pi
            if m == 0:
                cgrad[b, 0, 0] = add_r
                cgrad[b, 0, 1] = add_i
            else:
                cgrad[b, 0, 0] += add_r
                cgrad[b, 0, 1] += add_i
        yield
        for k in range(2):
            for ri in range(2):
                value = jnp.concatenate([cgrad[b, k, ri], jnp.zeros((8, size), F32)], 0)
                value = pltpu.roll(value, ahead, 0)
                value = jnp.concatenate([value, jnp.zeros_like(value)], 1)
                acc[k, ri, pl.ds(base, tall), :] += pltpu.roll(value, column, 1)

    def together(slot_ids):
        streams = [window(b, slot) for b, slot in enumerate(slot_ids)]
        while streams:
            for stream in list(streams):
                try:
                    next(stream)
                except StopIteration:
                    streams.remove(stream)

    for copy in facts_in:
        copy.wait()

    def is_here(slot, last):
        row = fact(slot, 0) - chip_top
        return jnp.logical_and(fact(slot, 2) > 0, jnp.logical_and(row >= 0, row <= last))

    def count_early(slot, count):
        return count + is_here(slot, limit).astype(jnp.int32)

    def choose(slot, carry):
        count, mine = carry
        if final:
            middle = jnp.logical_and(slot >= 2 * slots, slot < 4 * slots)
            early = jnp.logical_and(middle, is_here(slot, limit))
            here = jnp.logical_and(is_here(slot, 2 * tile - 1), jnp.logical_not(early))
        else:
            here = is_here(slot, limit)
        taken = jnp.logical_and(here, lax.rem(count, 2) == core)

        @pl.when(taken)
        def _():
            todo[mine] = slot

        return count + here.astype(jnp.int32), mine + taken.astype(jnp.int32)

    zero = jnp.int32(0)
    if final:
        count = lax.fori_loop(2 * slots, 4 * slots, count_early, zero)
        _, number = lax.fori_loop(0, 6 * slots, choose, (count, zero))
    else:
        _, number = lax.fori_loop(2 * slots, 4 * slots, choose, (zero, zero))
    move.wait()

    def two(i, carry):
        together([todo[2 * i], todo[2 * i + 1]])
        return carry

    lax.fori_loop(0, lax.div(number, 2), two, 0)

    @pl.when(lax.rem(number, 2) == 1)
    def _():
        together([todo[number - 1]])

    if final:
        mine_ref, theirs_ref = outs
        move(acc.at[:, :, pl.ds(top, tile)], mine_ref)
        move(acc.at[:, :, pl.ds(other, tile)], theirs_ref.at[:, :, pl.ds(0, tile)])
        move(acc.at[:, :, pl.ds(2 * tile, size)], theirs_ref.at[:, :, pl.ds(tile, size)])
    else:
        move(acc.at[:, :, pl.ds(0, 2 * tile)], outs[0])
    move.wait()


def flat_kernel(size, modes, slots, tile, final, n_pats, *refs):
    place, own, pair = refs[:3]
    pats, rest = refs[3:3 + n_pats], refs[3 + n_pats:]
    n_before, n_outs = (2, 2) if final else (0, 1)
    before, rest = rest[:n_before], rest[n_before:]
    inputs, rest = rest[:3], rest[3:]
    outs, sums_ref, scratch = rest[:n_outs], rest[n_outs], rest[n_outs + 1:]
    kernel(size, modes, slots, tile, final, place, own, pair, pats, before, *inputs, outs, sums_ref, *scratch)


def windows(place, own, pair, pats, before, waves, prop, table, slots):
    modes, _, size, _ = waves.shape
    tile, columns = own.shape[2:]
    final = bool(before)
    sums = jax.ShapeDtypeStruct((2 * modes * size + LOSS_PAD, size), F32)
    if final:
        outs = (
            jax.ShapeDtypeStruct((2, 2, tile, columns), F32),
            jax.ShapeDtypeStruct((2, 2, tile + size, columns), F32),
        )
    else:
        outs = (jax.ShapeDtypeStruct((2, 2, 2 * tile, columns), F32),)
    expected = (4 if final else 2) * modes * 6 * 16 * size**3
    return pl.pallas_call(
        functools.partial(flat_kernel, size, modes, slots, tile, final, len(pats)),
        out_shape=outs + (sums,),
        in_specs=[SMEM] + [HBM] * (2 + len(pats) + len(before)) + [VMEM] * 3,
        out_specs=(HBM,) * len(outs) + (VMEM,),
        scratch_shapes=[
            pltpu.VMEM((2, 2, 2 * tile + size, columns), F32),
            pltpu.VMEM((2, 2, 2 * tile + size, columns), F32),
            pltpu.VMEM((len(pats), slots * size, size), F32),
            pltpu.SMEM((len(pats), 8, size), F32),
            pltpu.SMEM((6 * slots,), jnp.int32),
            pltpu.VMEM((2, 6 * size, 2 * size), BF16),
            pltpu.VMEM((2, 2, 2, size, size), F32),
            pltpu.VMEM((2, 2, 2, size, size), F32),
            pltpu.VMEM((2, modes, 2, size, size), F32),
            pltpu.VMEM((2, modes, 2, size, size), F32),
            pltpu.VMEM((2, 12, 2, modes * size, 2 * size), BF16),
            pltpu.SemaphoreType.DMA((48,)),
        ],
        compiler_params=pltpu.CompilerParams(vmem_limit_bytes=48 * 1024 * 1024),
        cost_estimate=pl.CostEstimate(flops=3 * expected, bytes_accessed=8 << 20, transcendentals=0),
    )(place, own, pair, *pats, *before, waves, prop, table)


def sum_over(value, axis, halo_of, finish):
    count = lax.axis_size(axis)
    index = lax.axis_index(axis)
    bits = [1 << i for i in range(count.bit_length() - 1)]
    cut, whole = bits[:2], bits[2:]
    halo = None
    for bit in cut:
        half = value.shape[0] // 2
        side = (index // bit) % 2
        kept = lax.dynamic_slice_in_dim(value, side * half, half, 0)
        given = lax.dynamic_slice_in_dim(value, (1 - side) * half, half, 0)
        value = kept + swapped(given, axis, bit)
        if halo is None:
            halo = halo_of()
    for step, bit in enumerate(whole):
        if step == len(whole) - 1:
            value, halo = lax.optimization_barrier((value, halo))
        value = value + swapped(value, axis, bit)
    value, done = lax.optimization_barrier((value, finish(halo)))
    for bit in cut[::-1]:
        side = (index // bit) % 2
        got = swapped(value, axis, bit)
        value = jnp.concatenate([jnp.where(side == 0, value, got), jnp.where(side == 0, got, value)], 0)
    return value, done


def shards(object_slices, probe_modes, propagator_phase, measured, positions, live_count):
    modes, _, size, _ = probe_modes.shape
    tile = object_slices.shape[2]
    slots = positions.shape[0]
    count = lax.axis_size("scan")
    index = lax.axis_index("scan")
    core = index % 2
    chip = index // 2
    place = jnp.stack([core, chip * 2 * tile, (chip - 1) * 2 * slots]).astype(jnp.int32)
    prop = jnp.stack([jnp.cos(propagator_phase), jnp.sin(propagator_phase)])
    table = jnp.asarray(fourier_table(size))
    pair = swapped(object_slices, "scan", 1)
    own_pat = pack_up(positions, live_count, measured)
    pair_pat = swapped(own_pat, "scan", 1)
    up_own = shifted(own_pat, "scan", 2)
    down_own = shifted(pack_down(place, own_pat, object_slices, pair), "scan", -2)
    before = windows(
        place, object_slices, pair, (own_pat, pair_pat), (), probe_modes, prop, table, slots
    )
    before, up_own, down_own = lax.optimization_barrier((before, up_own, down_own))
    up_pair = swapped(up_own, "scan", 1)
    down_pair = swapped(down_own, "scan", 1)
    mine, theirs, sums = windows(
        place, object_slices, pair, (up_own, up_pair, own_pat, pair_pat, down_own, down_pair), before,
        probe_modes, prop, table, slots,
    )
    back = swapped(theirs, "scan", 1)

    def send_halo():
        halo = theirs[:, :, tile:] + back[:, :, tile:]
        return lax.ppermute(halo, "scan", [(s, s + 1) for s in range(1, count - 1, 2)])

    def finish(halo):
        return mine + back[:, :, :tile] + jnp.pad(halo, ((0, 0), (0, 0), (0, tile - size), (0, 0)))

    sums, grad = sum_over(sums, "scan", send_halo, finish)
    mode_rows = 2 * modes * size
    probe_gradient = sums[:mode_rows].reshape(probe_modes.shape)
    losses = sums[mode_rows:mode_rows + 8].reshape(-1)
    position_loss = lax.dynamic_slice_in_dim(losses, index * slots, slots, 0)
    return (grad, probe_gradient, position_loss)


def solution(mesh):
    return jax.shard_map(
        shards,
        mesh=mesh,
        in_specs=(
            P("parts", None, "scan", None),
            P("parts", None, None, None),
            P(),
            P(("parts", "scan"), None, None),
            P(("parts", "scan"), None),
            P(("parts", "scan")),
        ),
        out_specs=(
            P("parts", None, "scan", None),
            P("parts", None, None, None),
            P(("parts", "scan")),
        ),
        check_vma=False,
    )
```

```python
import functools
import math

import jax
import jax.numpy as jnp
import numpy as np
from jax import lax
from jax.experimental import pallas as pl
from jax.experimental.pallas import tpu as pltpu
from jax.sharding import PartitionSpec as P

F32 = jnp.float32
BF16 = jnp.bfloat16
LOSS_PAD = 16
VMEM_LIMIT = 48 * 1024 * 1024
HBM = pl.BlockSpec(memory_space=pl.ANY)
VMEM = pl.BlockSpec(memory_space=pltpu.VMEM)
SMEM = pl.BlockSpec(memory_space=pltpu.SMEM)


def shifted(value, axis, steps):
    count = lax.axis_size(axis)
    first, last = (max(0, -steps), min(count, count - steps))
    return lax.ppermute(value, axis, [(source, source + steps) for source in range(first, last)])


def swapped(value, axis, bit):
    count = lax.axis_size(axis)
    return lax.ppermute(value, axis, [(source, source ^ bit) for source in range(count)])


def fourier_table(size):
    counter = np.arange(size)
    angles = (counter[:, None] * counter[None, :] % size) * (2.0 * math.pi / size)
    return np.stack([np.cos(angles), np.sin(angles)]).astype(np.float32) / np.float32(math.sqrt(size))


class Mover:
    def __init__(self, sem):
        self.sem, self.copies, self.used = sem, [], 0

    def __call__(self, source, target):
        copy = pltpu.make_async_copy(source, target, self.sem.at[self.used])
        copy.start()
        self.copies.append(copy)
        self.used += 1

    def wait(self):
        for copy in self.copies:
            copy.wait()
        self.copies = []


def facts_kernel(slots, corners, live, measured, out):
    rows, size = measured.shape
    out[:rows] = measured[...]
    lane = lax.broadcasted_iota(jnp.int32, (8, size), 1)
    line = lax.broadcasted_iota(jnp.int32, (8, size), 0)
    value = jnp.zeros((8, size), jnp.int32)
    for s in range(slots):
        alive = (live[0] > s).astype(jnp.int32)
        fact = jnp.where(lane == 0, corners[0, s], jnp.where(lane == 1, corners[1, s], alive))
        value = jnp.where(jnp.logical_and(line == s, lane < 3), fact, value)
    out[rows:] = value.astype(F32)


def add_halo_kernel(place, packed, own, pair, out, sem):
    rows, size = packed.shape
    half = size // 2
    core = place[0]
    for source, side in ((own, 0), (pair, 1)):

        @pl.when(core == side)
        def _():
            move = Mover(sem)
            for k in range(2):
                for ri in range(2):
                    for lanes in range(2):
                        block = pl.ds(rows + ((k * 2 + ri) * 2 + lanes) * half, half)
                        move(source.at[k, ri, pl.ds(side * half, half), pl.ds(lanes * size, size)], out.at[block])
            out[:rows] = packed[...]
            move.wait()


def with_facts(positions, live, pattern):
    rows, size = pattern.shape
    return pl.pallas_call(
        functools.partial(facts_kernel, positions.shape[0]),
        out_shape=jax.ShapeDtypeStruct((rows + 8, size), F32),
        in_specs=[SMEM, SMEM, VMEM],
        out_specs=VMEM,
    )(positions.T, live, pattern)


def add_halo(place, packed, own, pair):
    rows, size = packed.shape
    return pl.pallas_call(
        add_halo_kernel,
        out_shape=jax.ShapeDtypeStruct((rows + 4 * size, size), F32),
        in_specs=[SMEM, VMEM, HBM, VMEM],
        out_specs=VMEM,
        scratch_shapes=[pltpu.SemaphoreType.DMA((8,))],
    )(place, packed, own, pair)


def kernel(
    early, size, modes, slots, tile, place, own, pair, packs, before, wave_ref, prop_ref, table_ref, outs, sums_ref,
    obj, acc, pat, written, whole, facts, todo, tables, cells, cgrad, wave1, far, ops, sem,
):
    core = place[0]
    chip_top = place[1]
    first_id = place[2]
    half = size // 2
    rows = slots * size
    top = pl.multiple_of(core * tile, tile)
    other = pl.multiple_of(tile - core * tile, tile)
    limit = 2 * tile - size
    first_group = 1 if early else 0

    move = Mover(sem)
    for i, source in enumerate(packs):
        move(source.at[pl.ds(rows, 8)], written.at[i])
    facts_in = move.copies
    move.copies = []
    move(own, obj.at[:, :, pl.ds(top, tile)])
    move(pair, obj.at[:, :, pl.ds(other, tile)])
    for i, source in enumerate(packs):
        move(source.at[pl.ds(0, rows)], pat.at[i])
    if early:
        acc[...] = jnp.zeros_like(acc)
        sums_ref[...] = jnp.zeros_like(sums_ref)
    else:
        for k in range(2):
            for ri in range(2):
                for side in range(2):
                    block = pl.ds(rows + 8 + ((k * 2 + ri) * 2 + side) * half, half)
                    lanes = pl.ds(side * size, size)
                    near = pl.multiple_of(2 * tile + core * half, half)
                    far_off = pl.multiple_of(2 * tile + half - core * half, half)
                    move(packs[4].at[block], obj.at[k, ri, pl.ds(near, half), lanes])
                    move(packs[5].at[block], obj.at[k, ri, pl.ds(far_off, half), lanes])
        old_grad, old_sums = before
        move(old_grad, acc.at[:, :, pl.ds(0, 2 * tile)])
        move(old_sums, sums_ref)
        acc[:, :, 2 * tile:] = jnp.zeros((2, 2, size, acc.shape[3]), F32)

    right_f, right_g, left_f, left_g = (tables.at[i] for i in range(4))
    cosine, sine = table_ref[0], table_ref[1]
    for index, part in enumerate(("high", "high", "low")):
        def cut(value):
            high = value.astype(BF16)
            return high if part == "high" else (value - high.astype(F32)).astype(BF16)
        c, s, n = cut(cosine), cut(sine), cut(-sine)
        base = index * 2 * size
        one, two = pl.ds(0, size), pl.ds(size, size)
        for kind, (a, b, d, e) in ((0, (c, n, s, c)), (1, (c, s, n, c))):
            tables[kind, pl.ds(base, size), one] = a
            tables[kind, pl.ds(base, size), two] = b
            tables[kind, pl.ds(base + size, size), one] = d
            tables[kind, pl.ds(base + size, size), two] = e

    def square(kind, part):
        return tables[kind, pl.ds(part * 2 * size, 2 * size), :]

    mat = functools.partial(jnp.dot, preferred_element_type=F32)
    (r1, l1, l2, r2, r3, l3, l4, r4, r5, l5, l6, r6) = range(12)
    pairs = range(modes // 2)

    def split(b, stage, at, value):
        high = value.astype(BF16)
        ops.at[b, stage, 0][at] = high
        ops.at[b, stage, 1][at] = (value - high.astype(F32)).astype(BF16)

    def put_right(b, stage, m, real, imag):
        split(b, stage, (pl.ds(m * size, size), pl.ds(0, size)), real)
        split(b, stage, (pl.ds(m * size, size), pl.ds(size, size)), imag)

    def right(b, stage, m, kind):
        at = (pl.ds(m * size, size), pl.ds(0, 2 * size))
        high, low = ops.at[b, stage, 0][at], ops.at[b, stage, 1][at]
        out = mat(jnp.concatenate([high, low, high], 1), tables[kind])
        return out[:, :size], out[:, size:]

    def put_left(b, stage, m, real, imag):
        base = (m // 2) * 2 * size
        lanes = pl.ds((m % 2) * size, size)
        split(b, stage, (pl.ds(base, size), lanes), real)
        split(b, stage, (pl.ds(base + size, size), lanes), imag)

    def left(b, stage, p, kind):
        at = (pl.ds(p * 2 * size, 2 * size), pl.ds(0, 2 * size))
        high, low = ops.at[b, stage, 0][at], ops.at[b, stage, 1][at]
        wide = jnp.concatenate([square(1 - kind, 0), square(1 - kind, 0), square(1 - kind, 2)], 1)
        out = mat(wide, jnp.concatenate([high, low, high], 0))
        return [(out[:size, j * size:(j + 1) * size], out[size:, j * size:(j + 1) * size]) for j in range(2)]

    def where_of(slot):
        group, owner, place_in = slot // (2 * slots), (slot // slots) % 2, slot % slots
        return 2 * (group - first_group) + (owner + core - 2 * owner * core), place_in

    def window(b, job):
        slot = todo[3 * job]
        row = todo[3 * job + 1]
        column = todo[3 * job + 2]
        base = pl.multiple_of(lax.div(row, 8) * 8, 8)
        ahead = row - base
        tall = size + 8
        for k in range(2):
            for ri in range(2):
                value = obj[k, ri, pl.ds(base, tall), :]
                value = pltpu.roll(value, 2 * size - column, 1)[:, :size]
                cells[b, k, ri] = pltpu.roll(value, tall - ahead, 0)[:size]
        yield
        for m in range(modes):
            pr, pi = wave_ref[m, 0], wave_ref[m, 1]
            o_r, o_i = cells[b, 0, 0], cells[b, 0, 1]
            put_right(b, r1, m, pr * o_r - pi * o_i, pr * o_i + pi * o_r)
        yield
        for m in range(modes):
            put_left(b, l1, m, *right(b, r1, m, 0))
        yield
        for p in pairs:
            for j, (re, im) in enumerate(left(b, l1, p, 0)):
                h_r, h_i = prop_ref[0], prop_ref[1]
                put_left(b, l2, 2 * p + j, re * h_r - im * h_i, re * h_i + im * h_r)
        yield
        for p in pairs:
            for j, (re, im) in enumerate(left(b, l2, p, 1)):
                put_right(b, r2, 2 * p + j, re, im)
        yield
        for m in range(modes):
            re, im = right(b, r2, m, 1)
            wave1[b, m, 0] = re
            wave1[b, m, 1] = im
            o_r, o_i = cells[b, 1, 0], cells[b, 1, 1]
            put_right(b, r3, m, re * o_r - im * o_i, re * o_i + im * o_r)
        yield
        for m in range(modes):
            put_left(b, l3, m, *right(b, r3, m, 0))
        yield
        for p in pairs:
            for j, (re, im) in enumerate(left(b, l3, p, 0)):
                far[b, 2 * p + j, 0] = re
                far[b, 2 * p + j, 1] = im
        yield
        total = jnp.zeros((size, size), F32)
        for m in range(modes):
            re, im = far[b, m, 0], far[b, m, 1]
            total = total + (re * re + im * im)
        buffer, line = where_of(slot)
        target = pat[buffer, pl.ds(pl.multiple_of(line * size, size), size), :]
        amplitude = jnp.sqrt(total + 0.5)
        residual = amplitude - target
        loss = 0.5 * jnp.sum(residual * residual) * (2.0 / (size * size))
        ratio = residual / amplitude
        spot = lax.broadcasted_iota(jnp.int32, (8, size), 0) * size + lax.broadcasted_iota(jnp.int32, (8, size), 1)
        for end in (1, 2):
            at = (pl.ds(end * modes * size + (end - 1) * LOSS_PAD, 8), pl.ds(0, size))
            sums_ref[at] = jnp.where(spot == first_id + slot, loss, sums_ref[at])
        for m in range(modes):
            put_left(b, l4, m, far[b, m, 0] * ratio, far[b, m, 1] * ratio)
        yield
        for p in pairs:
            for j, (re, im) in enumerate(left(b, l4, p, 1)):
                put_right(b, r4, 2 * p + j, re, im)
        yield
        for m in range(modes):
            re, im = right(b, r4, m, 1)
            w_r, w_i = wave1[b, m, 0], wave1[b, m, 1]
            add_r, add_i = re * w_r + im * w_i, im * w_r - re * w_i
            if m == 0:
                cgrad[b, 1, 0] = add_r
                cgrad[b, 1, 1] = add_i
            else:
                cgrad[b, 1, 0] += add_r
                cgrad[b, 1, 1] += add_i
            o_r, o_i = cells[b, 1, 0], cells[b, 1, 1]
            put_right(b, r5, m, re * o_r + im * o_i, im * o_r - re * o_i)
        yield
        for m in range(modes):
            put_left(b, l5, m, *right(b, r5, m, 0))
        yield
        for p in pairs:
            for j, (re, im) in enumerate(left(b, l5, p, 0)):
                h_r, h_i = prop_ref[0], prop_ref[1]
                put_left(b, l6, 2 * p + j, re * h_r + im * h_i, im * h_r - re * h_i)
        yield
        for p in pairs:
            for j, (re, im) in enumerate(left(b, l6, p, 1)):
                put_right(b, r6, 2 * p + j, re, im)
        yield
        for m in range(modes):
            re, im = right(b, r6, m, 1)
            o_r, o_i = cells[b, 0, 0], cells[b, 0, 1]
            line = 2 * m * size + (2 * m // modes) * LOSS_PAD
            sums_ref[pl.ds(line, size), :] += re * o_r + im * o_i
            sums_ref[pl.ds(line + size, size), :] += im * o_r - re * o_i
            pr, pi = wave_ref[m, 0], wave_ref[m, 1]
            add_r, add_i = re * pr + im * pi, im * pr - re * pi
            if m == 0:
                cgrad[b, 0, 0] = add_r
                cgrad[b, 0, 1] = add_i
            else:
                cgrad[b, 0, 0] += add_r
                cgrad[b, 0, 1] += add_i
        yield
        for k in range(2):
            for ri in range(2):
                value = jnp.concatenate([cgrad[b, k, ri], jnp.zeros((8, size), F32)], 0)
                value = pltpu.roll(value, ahead, 0)
                value = jnp.concatenate([value, jnp.zeros_like(value)], 1)
                acc[k, ri, pl.ds(base, tall), :] += pltpu.roll(value, column, 1)

    def together(jobs):
        streams = [window(*job) for job in jobs]
        while streams:
            for stream in list(streams):
                try:
                    next(stream)
                except StopIteration:
                    streams.remove(stream)

    for copy in facts_in:
        copy.wait()
    whole[...] = written[...].astype(jnp.int32)
    move(whole, facts)
    move.copies.pop().wait()
    count = jnp.int32(0)
    number = jnp.int32(0)
    wanted = []
    for slot in range(2 * slots if early else 0, 4 * slots if early else 6 * slots):
        buffer, line = where_of(slot)
        row = facts[buffer, line, 0] - chip_top
        alive = jnp.logical_and(facts[buffer, line, 2] > 0, row >= 0)
        first = jnp.logical_and(alive, row <= limit).astype(jnp.int32)
        here = first if early else jnp.logical_and(alive, row < 2 * tile).astype(jnp.int32)
        if not early and 2 * slots <= slot < 4 * slots:
            here = here - first
            count = count + first
        wanted.append((slot, row, facts[buffer, line, 1], here))
    for slot, row, column, here in wanted:
        todo[3 * number] = jnp.int32(slot)
        todo[3 * number + 1] = row
        todo[3 * number + 2] = column
        number = number + here * (1 - lax.bitwise_xor(lax.bitwise_and(count, 1), core))
        count = count + here
    move.wait()

    def two(step, carry):
        together([(b, 2 * step + b) for b in range(2)])
        return carry

    lax.fori_loop(0, lax.div(number, 2), two, 0)

    @pl.when(lax.bitwise_and(number, 1) == 1)
    def _():
        together([(0, number - 1)])

    if early:
        move(acc.at[:, :, pl.ds(0, 2 * tile)], outs[0])
    else:
        mine_ref, theirs_ref = outs
        move(acc.at[:, :, pl.ds(top, tile)], mine_ref)
        move(acc.at[:, :, pl.ds(other, tile)], theirs_ref.at[:, :, pl.ds(0, tile)])
        move(acc.at[:, :, pl.ds(2 * tile, size)], theirs_ref.at[:, :, pl.ds(tile, size)])
    move.wait()


def flat_kernel(early, size, modes, slots, tile, counts, *refs):
    groups = []
    for count in counts:
        groups.append(refs[:count])
        refs = refs[count:]
    fixed, packs, before, inputs, outs, sums, scratch = groups
    kernel(early, size, modes, slots, tile, *fixed, packs, before, *inputs, outs, *sums, *scratch)


def windows(place, own, pair, packs, before, waves, prop, table, slots):
    modes, _, size, _ = waves.shape
    tile, columns = own.shape[2:]
    early = not before
    sums = jax.ShapeDtypeStruct((2 * modes * size + 2 * LOSS_PAD, size), F32)
    if early:
        outs = (jax.ShapeDtypeStruct((2, 2, 2 * tile, columns), F32),)
    else:
        outs = (
            jax.ShapeDtypeStruct((2, 2, tile, columns), F32),
            jax.ShapeDtypeStruct((2, 2, tile + size, columns), F32),
        )
    scratch = [
        pltpu.VMEM((2, 2, 2 * tile + size, columns), F32),
        pltpu.VMEM((2, 2, 2 * tile + size, columns), F32),
        pltpu.VMEM((len(packs), slots * size, size), F32),
        pltpu.VMEM((len(packs), 8, size), F32),
        pltpu.VMEM((len(packs), 8, size), jnp.int32),
        pltpu.SMEM((len(packs), 8, size), jnp.int32),
        pltpu.SMEM((9 * slots + 8,), jnp.int32),
        pltpu.VMEM((2, 6 * size, 2 * size), BF16),
        pltpu.VMEM((2, 2, 2, size, size), F32),
        pltpu.VMEM((2, 2, 2, size, size), F32),
        pltpu.VMEM((2, modes, 2, size, size), F32),
        pltpu.VMEM((2, modes, 2, size, size), F32),
        pltpu.VMEM((2, 12, 2, modes * size, 2 * size), BF16),
        pltpu.SemaphoreType.DMA((48,)),
    ]
    counts = (3, len(packs), len(before), 3, len(outs), 1, len(scratch))
    return pl.pallas_call(
        functools.partial(flat_kernel, early, size, modes, slots, tile, counts),
        out_shape=outs + (sums,),
        in_specs=[SMEM] + [HBM] * (2 + len(packs) + len(before)) + [VMEM] * 3,
        out_specs=(HBM,) * len(outs) + (VMEM,),
        scratch_shapes=scratch,
        compiler_params=pltpu.CompilerParams(vmem_limit_bytes=VMEM_LIMIT),
        cost_estimate=pl.CostEstimate(flops=6 * modes * 6 * 16 * size**3, bytes_accessed=8 << 20, transcendentals=0),
    )(place, own, pair, *packs, *before, waves, prop, table)


def swapped_beside(value, axis, bit, work):
    return lax.optimization_barrier((swapped(value, axis, bit), work))


def halves(value, axis, bit):
    half = value.shape[0] // 2
    side = (lax.axis_index(axis) // bit) % 2
    kept = lax.dynamic_slice_in_dim(value, side * half, half, 0)
    given = lax.dynamic_slice_in_dim(value, (1 - side) * half, half, 0)
    return kept, given


def in_order(value, got, axis, bit):
    side = (lax.axis_index(axis) // bit) % 2
    return jnp.where(side == 0, value, got), jnp.where(side == 0, got, value)


def shards(object_slices, probe_modes, propagator_phase, measured, positions, live_count):
    modes, _, size, _ = probe_modes.shape
    tile = object_slices.shape[2]
    slots = positions.shape[0]
    count = lax.axis_size("scan")
    index = lax.axis_index("scan")
    core = index % 2
    chip = index // 2
    place = jnp.stack([core, chip * 2 * tile, (chip - 1) * 2 * slots]).astype(jnp.int32)
    prop = jnp.stack([jnp.cos(propagator_phase), jnp.sin(propagator_phase)])
    table = jnp.asarray(fourier_table(size))
    pattern = measured.reshape(slots * size, size)
    pair = swapped(object_slices, "scan", 1)
    packed = with_facts(positions, live_count, pattern)
    up = shifted(packed, "scan", 2)
    pair_packed = swapped(packed, "scan", 1)
    down = shifted(add_halo(place, packed, object_slices, pair), "scan", -2)
    shared = (probe_modes, prop, table, slots)
    before = windows(place, object_slices, pair, (packed, pair_packed), (), *shared)
    before, up, down = lax.optimization_barrier((before, up, down))
    packs = (up, swapped(up, "scan", 1), packed, pair_packed, down, swapped(down, "scan", 1))
    mine, theirs, sums = windows(place, object_slices, pair, packs, before, *shared)

    kept, given = halves(sums, "scan", 1)
    sums = kept + swapped(given, "scan", 1)
    back = swapped(theirs, "scan", 1)
    halo = theirs[:, :, tile:] + back[:, :, tile:]
    kept, given = halves(sums, "scan", 2)
    got, halo = swapped_beside(given, "scan", 2, halo)
    sums = kept + got
    halo = lax.ppermute(halo, "scan", [(s, s + 1) for s in range(1, count - 1, 2)])
    grad = mine + back[:, :, :tile] + jnp.pad(halo, ((0, 0), (0, 0), (0, tile - size), (0, 0)))
    bit = 4
    while bit < count:
        if 2 * bit < count:
            got = swapped(sums, "scan", bit)
        else:
            got, grad = swapped_beside(sums, "scan", bit, grad)
        sums = sums + got
        bit *= 2
    sums = jnp.concatenate(in_order(sums, swapped(sums, "scan", 2), "scan", 2), 0)
    half = modes * size
    losses = sums[half:half + 8].reshape(-1)
    position_loss = lax.dynamic_slice_in_dim(losses, index * slots, slots, 0)
    sums = sums[:half]
    got, position_loss = swapped_beside(sums, "scan", 1, position_loss)
    probe_gradient = jnp.concatenate(in_order(sums, got, "scan", 1), 0).reshape(probe_modes.shape)
    return (grad, probe_gradient, position_loss)


def solution(mesh):
    return jax.shard_map(
        shards,
        mesh=mesh,
        in_specs=(
            P("parts", None, "scan", None),
            P("parts", None, None, None),
            P(),
            P(("parts", "scan"), None, None),
            P(("parts", "scan"), None),
            P(("parts", "scan")),
        ),
        out_specs=(
            P("parts", None, "scan", None),
            P("parts", None, None, None),
            P(("parts", "scan")),
        ),
        check_vma=False,
    )
```

```python
import functools
import math

import jax
import jax.numpy as jnp
import numpy as np
from jax import lax
from jax.experimental import pallas as pl
from jax.experimental.pallas import tpu as pltpu
from jax.sharding import PartitionSpec as P

F32 = jnp.float32
BF16 = jnp.bfloat16
LOSS_PAD = 16
VMEM_LIMIT = 48 * 1024 * 1024
HBM = pl.BlockSpec(memory_space=pl.ANY)
VMEM = pl.BlockSpec(memory_space=pltpu.VMEM)
SMEM = pl.BlockSpec(memory_space=pltpu.SMEM)


def shifted(value, axis, steps):
    count = lax.axis_size(axis)
    first, last = (max(0, -steps), min(count, count - steps))
    return lax.ppermute(value, axis, [(source, source + steps) for source in range(first, last)])


def swapped(value, axis, bit):
    count = lax.axis_size(axis)
    return lax.ppermute(value, axis, [(source, source ^ bit) for source in range(count)])


def fourier_table(size):
    counter = np.arange(size)
    angles = (counter[:, None] * counter[None, :] % size) * (2.0 * math.pi / size)
    return np.stack([np.cos(angles), np.sin(angles)]).astype(np.float32) / np.float32(math.sqrt(size))


class Mover:
    def __init__(self, sem):
        self.sem, self.copies, self.used = sem, [], 0

    def __call__(self, source, target):
        copy = pltpu.make_async_copy(source, target, self.sem.at[self.used])
        copy.start()
        self.copies.append(copy)
        self.used += 1

    def wait(self):
        for copy in self.copies:
            copy.wait()
        self.copies = []


def facts_kernel(slots, corners, live, measured, out):
    rows, size = measured.shape
    out[:rows] = measured[...]
    lane = lax.broadcasted_iota(jnp.int32, (8, size), 1)
    line = lax.broadcasted_iota(jnp.int32, (8, size), 0)
    value = jnp.zeros((8, size), jnp.int32)
    for s in range(slots):
        alive = (live[0] > s).astype(jnp.int32)
        fact = jnp.where(lane == 0, corners[0, s], jnp.where(lane == 1, corners[1, s], alive))
        value = jnp.where(jnp.logical_and(line == s, lane < 3), fact, value)
    out[rows:] = value.astype(F32)


def add_halo_kernel(place, packed, own, pair, out, sem):
    rows, size = packed.shape
    half = size // 2
    core = place[0]
    for source, side in ((own, 0), (pair, 1)):

        @pl.when(core == side)
        def _():
            move = Mover(sem)
            for k in range(2):
                for ri in range(2):
                    for lanes in range(2):
                        block = pl.ds(rows + ((k * 2 + ri) * 2 + lanes) * half, half)
                        move(source.at[k, ri, pl.ds(side * half, half), pl.ds(lanes * size, size)], out.at[block])
            out[:rows] = packed[...]
            move.wait()


def with_facts(positions, live, pattern):
    rows, size = pattern.shape
    return pl.pallas_call(
        functools.partial(facts_kernel, positions.shape[0]),
        out_shape=jax.ShapeDtypeStruct((rows + 8, size), F32),
        in_specs=[SMEM, SMEM, VMEM],
        out_specs=VMEM,
    )(positions.T, live, pattern)


def add_halo(place, packed, own, pair):
    rows, size = packed.shape
    return pl.pallas_call(
        add_halo_kernel,
        out_shape=jax.ShapeDtypeStruct((rows + 4 * size, size), F32),
        in_specs=[SMEM, VMEM, HBM, VMEM],
        out_specs=VMEM,
        scratch_shapes=[pltpu.SemaphoreType.DMA((8,))],
    )(place, packed, own, pair)


def kernel(
    early, size, modes, slots, tile, place, own, pair, packs, before, wave_ref, prop_ref, table_ref, outs, sums_ref,
    obj, acc, pat, written, whole, facts, todo, tables, cells, cgrad, wave1, far, ops, sem,
):
    core = place[0]
    chip_top = place[1]
    first_id = place[2]
    half = size // 2
    rows = slots * size
    top = pl.multiple_of(core * tile, tile)
    other = pl.multiple_of(tile - core * tile, tile)
    limit = 2 * tile - size
    first_group = 1 if early else 0

    move = Mover(sem)
    for i, source in enumerate(packs):
        move(source.at[pl.ds(rows, 8)], written.at[i])
    facts_in = move.copies
    move.copies = []
    move(own, obj.at[:, :, pl.ds(top, tile)])
    move(pair, obj.at[:, :, pl.ds(other, tile)])
    for i, source in enumerate(packs):
        move(source.at[pl.ds(0, rows)], pat.at[i])
    if early:
        acc[...] = jnp.zeros_like(acc)
        sums_ref[...] = jnp.zeros_like(sums_ref)
    else:
        for k in range(2):
            for ri in range(2):
                for side in range(2):
                    block = pl.ds(rows + 8 + ((k * 2 + ri) * 2 + side) * half, half)
                    lanes = pl.ds(side * size, size)
                    near = pl.multiple_of(2 * tile + core * half, half)
                    far_off = pl.multiple_of(2 * tile + half - core * half, half)
                    move(packs[4].at[block], obj.at[k, ri, pl.ds(near, half), lanes])
                    move(packs[5].at[block], obj.at[k, ri, pl.ds(far_off, half), lanes])
        move(before[0], sums_ref)
        acc[...] = jnp.zeros_like(acc)

    right_f, right_g, left_f, left_g = (tables.at[i] for i in range(4))
    cosine, sine = table_ref[0], table_ref[1]
    for index, part in enumerate(("high", "high", "low")):
        def cut(value):
            high = value.astype(BF16)
            return high if part == "high" else (value - high.astype(F32)).astype(BF16)
        c, s, n = cut(cosine), cut(sine), cut(-sine)
        base = index * 2 * size
        one, two = pl.ds(0, size), pl.ds(size, size)
        for kind, (a, b, d, e) in ((0, (c, n, s, c)), (1, (c, s, n, c))):
            tables[kind, pl.ds(base, size), one] = a
            tables[kind, pl.ds(base, size), two] = b
            tables[kind, pl.ds(base + size, size), one] = d
            tables[kind, pl.ds(base + size, size), two] = e

    def square(kind, part):
        return tables[kind, pl.ds(part * 2 * size, 2 * size), :]

    mat = functools.partial(jnp.dot, preferred_element_type=F32)
    (r1, l1, l2, r2, r3, l3, l4, r4, r5, l5, l6, r6) = range(12)
    pairs = range(modes // 2)

    def split(b, stage, at, value):
        high = value.astype(BF16)
        ops.at[b, stage, 0][at] = high
        ops.at[b, stage, 1][at] = (value - high.astype(F32)).astype(BF16)

    def put_right(b, stage, m, real, imag):
        split(b, stage, (pl.ds(m * size, size), pl.ds(0, size)), real)
        split(b, stage, (pl.ds(m * size, size), pl.ds(size, size)), imag)

    def right(b, stage, m, kind):
        at = (pl.ds(m * size, size), pl.ds(0, 2 * size))
        high, low = ops.at[b, stage, 0][at], ops.at[b, stage, 1][at]
        out = mat(jnp.concatenate([high, low, high], 1), tables[kind])
        return out[:, :size], out[:, size:]

    def put_left(b, stage, m, real, imag):
        base = (m // 2) * 2 * size
        lanes = pl.ds((m % 2) * size, size)
        split(b, stage, (pl.ds(base, size), lanes), real)
        split(b, stage, (pl.ds(base + size, size), lanes), imag)

    def left(b, stage, p, kind):
        at = (pl.ds(p * 2 * size, 2 * size), pl.ds(0, 2 * size))
        high, low = ops.at[b, stage, 0][at], ops.at[b, stage, 1][at]
        wide = jnp.concatenate([square(1 - kind, 0), square(1 - kind, 0), square(1 - kind, 2)], 1)
        out = mat(wide, jnp.concatenate([high, low, high], 0))
        return [(out[:size, j * size:(j + 1) * size], out[size:, j * size:(j + 1) * size]) for j in range(2)]

    def where_of(slot):
        group, owner, place_in = slot // (2 * slots), (slot // slots) % 2, slot % slots
        return 2 * (group - first_group) + (owner + core - 2 * owner * core), place_in

    def window(b, job):
        slot = todo[3 * job]
        row = todo[3 * job + 1]
        column = todo[3 * job + 2]
        base = pl.multiple_of(lax.div(row, 8) * 8, 8)
        ahead = row - base
        tall = size + 8
        for k in range(2):
            for ri in range(2):
                value = obj[k, ri, pl.ds(base, tall), :]
                value = pltpu.roll(value, 2 * size - column, 1)[:, :size]
                cells[b, k, ri] = pltpu.roll(value, tall - ahead, 0)[:size]
        yield
        for m in range(modes):
            pr, pi = wave_ref[m, 0], wave_ref[m, 1]
            o_r, o_i = cells[b, 0, 0], cells[b, 0, 1]
            put_right(b, r1, m, pr * o_r - pi * o_i, pr * o_i + pi * o_r)
        yield
        for m in range(modes):
            put_left(b, l1, m, *right(b, r1, m, 0))
        yield
        for p in pairs:
            for j, (re, im) in enumerate(left(b, l1, p, 0)):
                h_r, h_i = prop_ref[0], prop_ref[1]
                put_left(b, l2, 2 * p + j, re * h_r - im * h_i, re * h_i + im * h_r)
        yield
        for p in pairs:
            for j, (re, im) in enumerate(left(b, l2, p, 1)):
                put_right(b, r2, 2 * p + j, re, im)
        yield
        for m in range(modes):
            re, im = right(b, r2, m, 1)
            wave1[b, m, 0] = re
            wave1[b, m, 1] = im
            o_r, o_i = cells[b, 1, 0], cells[b, 1, 1]
            put_right(b, r3, m, re * o_r - im * o_i, re * o_i + im * o_r)
        yield
        for m in range(modes):
            put_left(b, l3, m, *right(b, r3, m, 0))
        yield
        for p in pairs:
            for j, (re, im) in enumerate(left(b, l3, p, 0)):
                far[b, 2 * p + j, 0] = re
                far[b, 2 * p + j, 1] = im
        yield
        total = jnp.zeros((size, size), F32)
        for m in range(modes):
            re, im = far[b, m, 0], far[b, m, 1]
            total = total + (re * re + im * im)
        buffer, line = where_of(slot)
        target = pat[buffer, pl.ds(pl.multiple_of(line * size, size), size), :]
        amplitude = jnp.sqrt(total + 0.5)
        residual = amplitude - target
        loss = 0.5 * jnp.sum(residual * residual) * (2.0 / (size * size))
        ratio = residual / amplitude
        spot = lax.broadcasted_iota(jnp.int32, (8, size), 0) * size + lax.broadcasted_iota(jnp.int32, (8, size), 1)
        for end in (1, 2):
            at = (pl.ds(end * modes * size + (end - 1) * LOSS_PAD, 8), pl.ds(0, size))
            sums_ref[at] = jnp.where(spot == first_id + slot, loss, sums_ref[at])
        for m in range(modes):
            put_left(b, l4, m, far[b, m, 0] * ratio, far[b, m, 1] * ratio)
        yield
        for p in pairs:
            for j, (re, im) in enumerate(left(b, l4, p, 1)):
                put_right(b, r4, 2 * p + j, re, im)
        yield
        for m in range(modes):
            re, im = right(b, r4, m, 1)
            w_r, w_i = wave1[b, m, 0], wave1[b, m, 1]
            add_r, add_i = re * w_r + im * w_i, im * w_r - re * w_i
            if m == 0:
                cgrad[b, 1, 0] = add_r
                cgrad[b, 1, 1] = add_i
            else:
                cgrad[b, 1, 0] += add_r
                cgrad[b, 1, 1] += add_i
            o_r, o_i = cells[b, 1, 0], cells[b, 1, 1]
            put_right(b, r5, m, re * o_r + im * o_i, im * o_r - re * o_i)
        yield
        for m in range(modes):
            put_left(b, l5, m, *right(b, r5, m, 0))
        yield
        for p in pairs:
            for j, (re, im) in enumerate(left(b, l5, p, 0)):
                h_r, h_i = prop_ref[0], prop_ref[1]
                put_left(b, l6, 2 * p + j, re * h_r + im * h_i, im * h_r - re * h_i)
        yield
        for p in pairs:
            for j, (re, im) in enumerate(left(b, l6, p, 1)):
                put_right(b, r6, 2 * p + j, re, im)
        yield
        for m in range(modes):
            re, im = right(b, r6, m, 1)
            o_r, o_i = cells[b, 0, 0], cells[b, 0, 1]
            line = 2 * m * size + (2 * m // modes) * LOSS_PAD
            sums_ref[pl.ds(line, size), :] += re * o_r + im * o_i
            sums_ref[pl.ds(line + size, size), :] += im * o_r - re * o_i
            pr, pi = wave_ref[m, 0], wave_ref[m, 1]
            add_r, add_i = re * pr + im * pi, im * pr - re * pi
            if m == 0:
                cgrad[b, 0, 0] = add_r
                cgrad[b, 0, 1] = add_i
            else:
                cgrad[b, 0, 0] += add_r
                cgrad[b, 0, 1] += add_i
        yield
        for k in range(2):
            for ri in range(2):
                value = jnp.concatenate([cgrad[b, k, ri], jnp.zeros((8, size), F32)], 0)
                value = pltpu.roll(value, ahead, 0)
                value = jnp.concatenate([value, jnp.zeros_like(value)], 1)
                acc[k, ri, pl.ds(base, tall), :] += pltpu.roll(value, column, 1)

    def together(jobs):
        streams = [window(*job) for job in jobs]
        while streams:
            for stream in list(streams):
                try:
                    next(stream)
                except StopIteration:
                    streams.remove(stream)

    for copy in facts_in:
        copy.wait()
    whole[...] = written[...].astype(jnp.int32)
    move(whole, facts)
    move.copies.pop().wait()
    count = jnp.int32(0)
    number = jnp.int32(0)
    wanted = []
    for slot in range(2 * slots if early else 0, 4 * slots if early else 6 * slots):
        buffer, line = where_of(slot)
        row = facts[buffer, line, 0] - chip_top
        alive = jnp.logical_and(facts[buffer, line, 2] > 0, row >= 0)
        first = jnp.logical_and(alive, row <= limit).astype(jnp.int32)
        here = first if early else jnp.logical_and(alive, row < 2 * tile).astype(jnp.int32)
        if not early and 2 * slots <= slot < 4 * slots:
            here = here - first
            count = count + first
        wanted.append((slot, row, facts[buffer, line, 1], here))
    for slot, row, column, here in wanted:
        todo[3 * number] = jnp.int32(slot)
        todo[3 * number + 1] = row
        todo[3 * number + 2] = column
        number = number + here * (1 - lax.bitwise_xor(lax.bitwise_and(count, 1), core))
        count = count + here
    move.wait()

    def two(step, carry):
        together([(b, 2 * step + b) for b in range(2)])
        return carry

    lax.fori_loop(0, lax.div(number, 2), two, 0)

    @pl.when(lax.bitwise_and(number, 1) == 1)
    def _():
        together([(0, number - 1)])

    if early:
        mine_ref, theirs_ref = outs
        move(acc.at[:, :, pl.ds(top, tile)], mine_ref)
        move(acc.at[:, :, pl.ds(other, tile)], theirs_ref)
    else:
        mine_ref, theirs_ref = outs
        move(acc.at[:, :, pl.ds(top, tile)], mine_ref)
        move(acc.at[:, :, pl.ds(other, tile)], theirs_ref.at[:, :, pl.ds(0, tile)])
        move(acc.at[:, :, pl.ds(2 * tile, size)], theirs_ref.at[:, :, pl.ds(tile, size)])
    move.wait()


def flat_kernel(early, size, modes, slots, tile, counts, *refs):
    groups = []
    for count in counts:
        groups.append(refs[:count])
        refs = refs[count:]
    fixed, packs, before, inputs, outs, sums, scratch = groups
    kernel(early, size, modes, slots, tile, *fixed, packs, before, *inputs, outs, *sums, *scratch)


def windows(place, own, pair, packs, before, waves, prop, table, slots):
    modes, _, size, _ = waves.shape
    tile, columns = own.shape[2:]
    early = not before
    sums = jax.ShapeDtypeStruct((2 * modes * size + 2 * LOSS_PAD, size), F32)
    if early:
        outs = (jax.ShapeDtypeStruct((2, 2, tile, columns), F32),) * 2
    else:
        outs = (
            jax.ShapeDtypeStruct((2, 2, tile, columns), F32),
            jax.ShapeDtypeStruct((2, 2, tile + size, columns), F32),
        )
    scratch = [
        pltpu.VMEM((2, 2, 2 * tile + size, columns), F32),
        pltpu.VMEM((2, 2, 2 * tile + size, columns), F32),
        pltpu.VMEM((len(packs), slots * size, size), F32),
        pltpu.VMEM((len(packs), 8, size), F32),
        pltpu.VMEM((len(packs), 8, size), jnp.int32),
        pltpu.SMEM((len(packs), 8, size), jnp.int32),
        pltpu.SMEM((9 * slots + 8,), jnp.int32),
        pltpu.VMEM((2, 6 * size, 2 * size), BF16),
        pltpu.VMEM((2, 2, 2, size, size), F32),
        pltpu.VMEM((2, 2, 2, size, size), F32),
        pltpu.VMEM((2, modes, 2, size, size), F32),
        pltpu.VMEM((2, modes, 2, size, size), F32),
        pltpu.VMEM((2, 12, 2, modes * size, 2 * size), BF16),
        pltpu.SemaphoreType.DMA((48,)),
    ]
    counts = (3, len(packs), len(before), 3, len(outs), 1, len(scratch))
    return pl.pallas_call(
        functools.partial(flat_kernel, early, size, modes, slots, tile, counts),
        out_shape=outs + (sums,),
        in_specs=[SMEM] + [HBM] * (2 + len(packs) + len(before)) + [VMEM] * 3,
        out_specs=(HBM,) * len(outs) + (VMEM,),
        scratch_shapes=scratch,
        compiler_params=pltpu.CompilerParams(vmem_limit_bytes=VMEM_LIMIT),
        cost_estimate=pl.CostEstimate(flops=6 * modes * 6 * 16 * size**3, bytes_accessed=8 << 20, transcendentals=0),
    )(place, own, pair, *packs, *before, waves, prop, table)


def swapped_beside(value, axis, bit, work):
    return lax.optimization_barrier((swapped(value, axis, bit), work))


def halves(value, axis, bit):
    half = value.shape[0] // 2
    side = (lax.axis_index(axis) // bit) % 2
    kept = lax.dynamic_slice_in_dim(value, side * half, half, 0)
    given = lax.dynamic_slice_in_dim(value, (1 - side) * half, half, 0)
    return kept, given


def in_order(value, got, axis, bit):
    side = (lax.axis_index(axis) // bit) % 2
    return jnp.where(side == 0, value, got), jnp.where(side == 0, got, value)


def shards(object_slices, probe_modes, propagator_phase, measured, positions, live_count):
    modes, _, size, _ = probe_modes.shape
    tile = object_slices.shape[2]
    slots = positions.shape[0]
    count = lax.axis_size("scan")
    index = lax.axis_index("scan")
    core = index % 2
    chip = index // 2
    place = jnp.stack([core, chip * 2 * tile, (chip - 1) * 2 * slots]).astype(jnp.int32)
    prop = jnp.stack([jnp.cos(propagator_phase), jnp.sin(propagator_phase)])
    table = jnp.asarray(fourier_table(size))
    pattern = measured.reshape(slots * size, size)
    pair = swapped(object_slices, "scan", 1)
    packed = with_facts(positions, live_count, pattern)
    up = shifted(packed, "scan", 2)
    pair_packed = swapped(packed, "scan", 1)
    down = shifted(add_halo(place, packed, object_slices, pair), "scan", -2)
    shared = (probe_modes, prop, table, slots)
    first_mine, first_theirs, first_sums = windows(place, object_slices, pair, (packed, pair_packed), (), *shared)
    first_theirs, first_sums, up, down = lax.optimization_barrier((first_theirs, first_sums, up, down))
    first_back = swapped(first_theirs, "scan", 1)
    packs = (up, swapped(up, "scan", 1), packed, pair_packed, down, swapped(down, "scan", 1))
    mine, theirs, sums = windows(place, object_slices, pair, packs, (first_sums,), *shared)

    kept, given = halves(sums, "scan", 1)
    sums = kept + swapped(given, "scan", 1)
    back = swapped(theirs, "scan", 1)
    halo = theirs[:, :, tile:] + back[:, :, tile:]
    kept, given = halves(sums, "scan", 2)
    got, halo = swapped_beside(given, "scan", 2, halo)
    sums = kept + got
    halo = lax.ppermute(halo, "scan", [(s, s + 1) for s in range(1, count - 1, 2)])
    grad = first_mine + first_back + mine + back[:, :, :tile] + jnp.pad(halo, ((0, 0), (0, 0), (0, tile - size), (0, 0)))
    bit = 4
    while bit < count:
        if 2 * bit < count:
            got = swapped(sums, "scan", bit)
        else:
            got, grad = swapped_beside(sums, "scan", bit, grad)
        sums = sums + got
        bit *= 2
    sums = jnp.concatenate(in_order(sums, swapped(sums, "scan", 2), "scan", 2), 0)
    half = modes * size
    losses = sums[half:half + 8].reshape(-1)
    position_loss = lax.dynamic_slice_in_dim(losses, index * slots, slots, 0)
    sums = sums[:half]
    got, position_loss = swapped_beside(sums, "scan", 1, position_loss)
    probe_gradient = jnp.concatenate(in_order(sums, got, "scan", 1), 0).reshape(probe_modes.shape)
    return (grad, probe_gradient, position_loss)


def solution(mesh):
    return jax.shard_map(
        shards,
        mesh=mesh,
        in_specs=(
            P("parts", None, "scan", None),
            P("parts", None, None, None),
            P(),
            P(("parts", "scan"), None, None),
            P(("parts", "scan"), None),
            P(("parts", "scan")),
        ),
        out_specs=(
            P("parts", None, "scan", None),
            P("parts", None, None, None),
            P(("parts", "scan")),
        ),
        check_vma=False,
    )
```
